32 devices in a mesh: kpt: 2 (over x), col: 16 (over z, y, core).
Axes of the slice: x: 2, y: 2, z: 4, core: 2. Of those that a mesh axis runs over, the one named last changes fastest.
Arguments:
- ancestor_rows: bfloat16 [4, 1024, 1024], P('kpt', 'col'), parts along dimension 0, may hold values from -0.375 to 0.375
- factor_rows: bfloat16 [80, 4, 64, 256], P('col', 'kpt'), parts along dimension 1, may hold values from -1.5 to 1.5
- pattern: int32 [80, 4], P('col'), may hold values from 0 to 15, as said below
- lengths: int32 [80], P('col'), may hold values from 2 to 4, as said below
- diag_inverse: float32 [80, 128, 128], P('col', 'kpt'), parts along dimension 1, may hold values from -6 to 6
- pole_weight: float32 [2], replicated, may hold values from 0.5 to 2
Outputs:
- inverse_row: bfloat16 [80, 4, 64, 256], P('col', 'kpt'), parts along dimension 1
- inverse_diag: float32 [80, 128, 128], P('col', 'kpt'), parts along dimension 1
- density: bfloat16 [80, 128, 256], P('col', 'kpt'), parts along dimension 1
The draws below stay inside these ranges and needn't reach their ends.
There are 2 independent parts, one for each index of `kpt`. The reference program is written for one: setup_inputs(seed, part) draws one part's arguments, and reference() takes and returns one part's arrays. A program takes and returns all parts, laid end to end along the dimension named above; an argument that names none is the same for every part. Nothing has to cross between parts.
Inputs may be any that keep to these rules, and one draw needn't show every extreme that they name: `pattern`: row k lists the ancestors of supernode k's structure; entries at positions lengths[k] or later are not used. The used entries of one row are distinct. Over the 5 supernodes of one device (aligned blocks of 5 rows), one ancestor is named by at most 2 used entries. `lengths`: the first supernode of each device's aligned block of 5 rows has 4 blocks.
All inputs are finite; a program needn't handle non-finite values.
Results may differ from the reference program's by a relative error of at most 0.0051.
Values may be sent and summed in bfloat16 or wider, within the bound.
A program may use at most 192 MiB of HBM per device.

```python
import jax
import jax.numpy as jnp
from jax import lax

B = 64
S = 4
POLES = 2
NK = 5
KS = 80
ANC = 16
N_COL = 16


def shared_layout(key):
    ancestor_count = N_COL
    surplus = ancestor_count // 16
    span_cells = S - 2
    excess = NK * S - ancestor_count - surplus
    key_common, key_device = jax.random.split(key)
    ordering = jax.random.permutation(key_common, ancestor_count)
    popular = ordering[:surplus]
    others = ordering[surplus:]

    def per_device(device_key):
        key_cells, key_popular, key_others = jax.random.split(device_key, 3)
        ranking = jax.random.permutation(key_cells, (NK - 1) * span_cells)
        removed = (ranking < excess).astype(jnp.int32).reshape(NK - 1, span_cells).sum(axis=1)
        removed = jnp.concatenate([jnp.zeros((1,), jnp.int32), removed])
        drawn_lengths = S - removed
        sequence = jnp.concatenate([jax.random.permutation(key_popular, popular), jax.random.permutation(key_others, others)])
        sequence = jnp.concatenate([sequence, sequence])
        starts = jnp.cumsum(drawn_lengths) - drawn_lengths
        places = starts[:, None] + jnp.arange(S)[None, :]
        return (drawn_lengths, sequence[places])
    drawn_lengths, entries = jax.vmap(per_device)(jax.random.split(key_device, ancestor_count))
    return (drawn_lengths.reshape(-1).astype(jnp.int32), entries.reshape(-1, S).astype(jnp.int32))


def draw_pattern(key, part):
    return shared_layout(key)[1]


def draw_lengths(key, part):
    return shared_layout(key)[0]


def levels(key, extent, cuts, smallest, high):
    def one(dim, parts):
        steps = jax.random.uniform(jax.random.fold_in(jax.random.fold_in(key, 6), dim), (parts,), jnp.float32, smallest / len(cuts), high / len(cuts))
        return jnp.repeat(jnp.exp(steps), extent[dim] // parts).reshape((-1,) + (1,) * (len(extent) - dim - 1))

    factor_of = one(*cuts[0])
    for cut in cuts[1:]:
        factor_of = factor_of * one(*cut)
    return factor_of


def centred(stream_key, shape, spread, reach, cuts=(), dtype=jnp.bfloat16):
    gain = levels(stream_key, shape, cuts, -0.22, 0.18) if cuts else 1.0
    values = jax.random.normal(stream_key, shape, jnp.float32) * spread * gain
    return jnp.minimum(jnp.maximum(values, -reach), reach).astype(dtype)


def setup_inputs(seed: int = 0, part: int = 0) -> dict:
    key_of = jax.random.split(jax.random.key(seed), 7)
    part_splits = jax.random.split(jax.random.fold_in(key_of[6], part), 7)
    ancestor_rows = centred(part_splits[0], (POLES, ANC * B, ANC * B), (S * B) ** -0.5, 0.375, ((1, 16),))
    factor_rows = centred(part_splits[1], (KS, POLES, B, S * B), 0.25, 1.5, ((0, 16),))
    pattern = draw_pattern(jax.random.fold_in(key_of[6], 71), part)
    lengths = draw_lengths(jax.random.fold_in(key_of[6], 71), part)
    diag_inverse = centred(part_splits[4], (KS, B, POLES * B), 1.0, 6.0, ((0, 16),), jnp.float32)
    pole_weight = jnp.clip(jax.random.uniform(key_of[5], (POLES,), jnp.float32, 0.5, 2.0), 0.5, 2.0)
    return {"ancestor_rows": ancestor_rows, "factor_rows": factor_rows, "pattern": pattern, "lengths": lengths, "diag_inverse": diag_inverse, "pole_weight": pole_weight}


def reference(ancestor_rows, factor_rows, pattern, lengths, diag_inverse, pole_weight):
    live_slots = jnp.arange(S)[None, :] < lengths[:, None]
    live_columns = jnp.repeat(live_slots, B, axis=1).astype(jnp.bfloat16)
    masked_factor = factor_rows * live_columns[:, None, None, :]
    row_blocks = ancestor_rows.reshape(POLES, ANC, B, ANC, B)

    def one_supernode(packed):
        factor_block, indices, live_rows = packed
        picked_rows = row_blocks[:, indices]
        picked = picked_rows[:, :, :, indices]
        products = jnp.einsum("pist,prjst->prij", factor_block.reshape(POLES, B, S, B).astype(jnp.float32),
                              picked.astype(jnp.float32), precision=lax.Precision.HIGHEST)
        rounded = products.astype(jnp.bfloat16)
        return rounded * live_rows.astype(jnp.bfloat16)[None, :, None, None]

    blocks_all = lax.map(one_supernode, (masked_factor, pattern, live_slots))
    supernodes = factor_rows.shape[0]
    column_blocks = jnp.transpose(blocks_all, (0, 1, 3, 2, 4)).reshape(supernodes, POLES, B, S * B)
    inverse_row = -column_blocks
    diagonal = jnp.einsum("kpic,kpjc->kipj", masked_factor.astype(jnp.float32), column_blocks.astype(jnp.float32),
                          precision=lax.Precision.HIGHEST)
    inverse_diag = diag_inverse + diagonal.reshape(supernodes, B, POLES * B)
    density = -jnp.einsum("p,kpic->kic", pole_weight, column_blocks.astype(jnp.float32),
                          precision=lax.Precision.HIGHEST)
    return inverse_row, inverse_diag, density.astype(jnp.bfloat16)
```

```python
import functools

import jax
import jax.numpy as jnp
from jax import lax
from jax.experimental import pallas as pl
from jax.experimental.pallas import tpu as pltpu
from jax.sharding import PartitionSpec as P

CAP = 2
MESH = pl.DeviceIdType.MESH
TABLE_BYTES = 16 * 2**20
VMEM_BYTES = 32 * 2**20
LEFT, RIGHT, ACROSS, TWIN = range(4)


def gather_kernel(
    line, lag,
    pattern, lengths, weight, anc, factor_hbm, diag_hbm,
    row_out, diag_out, density_out,
    *scratch,
):
    poles, width, span = anc.shape
    tables = scratch[:poles]
    factor, diag, spread, partial, send_sem, recv_sem, local_sem = scratch[poles:]
    supernodes = factor.shape[0]
    blocks = pattern.shape[1]
    me = lax.axis_index("col")
    core, row, z = me % 2, (me // 2) % 2, me // 4

    def index(at_z, at_row, at_core):
        return (at_z * 2 + at_row) * 2 + at_core

    targets = {
        LEFT: index(z - 1, row, core),
        RIGHT: index(z + 1, row, core),
        ACROSS: index(z, 1 - row, core),
        TWIN: index(z, row, 1 - core),
    }
    has = {LEFT: z > 0, RIGHT: z < line - 1}

    factor_in = pltpu.make_async_copy(factor_hbm, factor, local_sem.at[0])
    diag_in = pltpu.make_async_copy(diag_hbm, diag, local_sem.at[1])
    factor_in.start()
    diag_in.start()
    for p in range(poles):
        for strip in range(span // (2 * width)):
            tables[p][me, strip] = anc[p, :, strip * 2 * width:(strip + 1) * 2 * width]

    barrier = pltpu.get_barrier_semaphore()

    def greet(way):
        pl.semaphore_signal(barrier, inc=1, device_id={"col": targets[way]}, device_id_type=MESH)

    greet(TWIN)
    greet(ACROSS)
    for way in (LEFT, RIGHT):
        pl.when(has[way])(functools.partial(greet, way))
    pl.semaphore_wait(barrier, 2 + has[LEFT].astype(jnp.int32) + has[RIGHT].astype(jnp.int32))

    def remote(way, origin, p, source):
        return pltpu.make_async_remote_copy(
            src_ref=source,
            dst_ref=tables[p].at[origin],
            send_sem=send_sem.at[way, origin, p],
            recv_sem=recv_sem.at[origin, p],
            device_id={"col": targets[way]},
            device_id_type=MESH,
        )

    def send(way, origin, p, source):
        remote(way, origin, p, source).start()

    def arrived(origin, p):
        remote(TWIN, origin, p, tables[p].at[origin]).wait_recv()

    def own(p):
        block = tables[p].at[me]
        for way in (LEFT, RIGHT):
            pl.when(has[way])(functools.partial(send, way, me, p, block))
        send(ACROSS, me, p, block)
        send(TWIN, me, p, block)

    def from_line(p, side, distance):
        at_z = z - distance if side == LEFT else z + distance
        inside = at_z >= 0 if side == LEFT else at_z < line
        onward = RIGHT if side == LEFT else LEFT

        @pl.when(inside)
        def _():
            origin = index(at_z, row, core)
            arrived(origin, p)
            block = tables[p].at[origin]
            pl.when(has[onward])(functools.partial(send, onward, origin, p, block))
            send(ACROSS, origin, p, block)
            send(TWIN, origin, p, block)

    def from_across(p, distance):
        for sign in (-1, 1) if distance else (1,):
            at_z = z + sign * distance

            @pl.when((at_z >= 0) & (at_z < line))
            def _():
                origin = index(at_z, 1 - row, core)
                arrived(origin, p)
                send(TWIN, origin, p, tables[p].at[origin])

    def from_twin(p):
        for at_z in range(line):
            for at_row in range(2):
                arrived(index(at_z, at_row, 1 - core), p)

    lane = lax.broadcasted_iota(jnp.int32, (width, 2 * width), 1)

    def prepare():
        for k in range(supernodes):
            length = jnp.full(lane.shape, lengths[k], jnp.int32)
            for p in range(poles):
                for s in range(blocks):
                    start = s // 2 * 2 * width
                    strip = factor[k, p, :, start:start + 2 * width].astype(jnp.float32)
                    half = jnp.full(lane.shape, lax.rem(pattern[k, s], 2), jnp.int32)
                    swapped = jnp.concatenate([strip[:, width:], strip[:, :width]], axis=1)
                    placed = jnp.where(half == s % 2, strip, swapped)
                    keep = (lane // width == half) & (s < length)
                    spread[k, p, :, s * 2 * width:(s + 1) * 2 * width] = jnp.where(
                        keep, placed, 0.0
                    ).astype(jnp.bfloat16)

    wide = lax.broadcasted_iota(jnp.int32, (width, blocks * width), 1)
    contract = (((1,), (1,)), ((), ()))

    def compute(p):
        for k in range(supernodes):
            strips = [lax.div(pattern[k, s], 2) for s in range(blocks)]
            picked = jnp.concatenate(
                [
                    jnp.concatenate([tables[p][pattern[k, r], strip] for strip in strips], axis=1)
                    for r in range(blocks)
                ],
                axis=0,
            )
            product = lax.dot_general(spread[k, p], picked, contract, preferred_element_type=jnp.float32)
            product = jnp.where(wide < jnp.full(wide.shape, lengths[k] * width, jnp.int32), product, 0.0)
            rounded = product.astype(jnp.bfloat16)
            held = rounded.astype(jnp.float32)
            row_out[k, p] = (-held).astype(jnp.bfloat16)
            term = lax.dot_general(factor[k, p], rounded, contract, preferred_element_type=jnp.float32)
            columns = slice(p * width, (p + 1) * width)
            diag_out[k, :, columns] = diag[k, :, columns] + term
            total = weight[p] * held
            if p > 0:
                total = partial[k] + total
            if p < poles - 1:
                partial[k] = total
            else:
                density_out[k] = (-total).astype(jnp.bfloat16)

    def stage(p, step):
        if 1 <= step < line:
            from_line(p, LEFT, step)
            from_line(p, RIGHT, step)
        if 1 <= step <= line:
            from_across(p, step - 1)
        if step == line + 1:
            from_twin(p)
            compute(p)

    for p in range(poles):
        own(p)
    factor_in.wait()
    diag_in.wait()
    prepare()
    for step in range(1, line + 2 + lag * (poles - 1)):
        for p in range(poles):
            stage(p, step - lag * p)

    def left_device(way, origin, p):
        remote(way, origin, p, tables[p].at[origin]).wait_send()

    for p in range(poles):
        for at_z in range(line):
            origin = index(at_z, row, core)
            pl.when(has[LEFT] & (at_z >= z))(functools.partial(left_device, LEFT, origin, p))
            pl.when(has[RIGHT] & (at_z <= z))(functools.partial(left_device, RIGHT, origin, p))
            left_device(ACROSS, origin, p)
            for at_row in range(2):
                left_device(TWIN, index(at_z, at_row, core), p)


def gathered(ancestor_rows, factor_rows, pattern, lengths, diag_inverse, pole_weight):
    supernodes, poles, width, span = factor_rows.shape
    n = lax.axis_size("col")
    blocks = pattern.shape[1]
    smem = pl.BlockSpec(memory_space=pltpu.SMEM)
    vmem = pl.BlockSpec(memory_space=pltpu.VMEM)
    anywhere = pl.BlockSpec(memory_space=pl.ANY)
    return pl.pallas_call(
        functools.partial(gather_kernel, n // 4, 1),
        out_shape=(
            jax.ShapeDtypeStruct(factor_rows.shape, jnp.bfloat16),
            jax.ShapeDtypeStruct(diag_inverse.shape, jnp.float32),
            jax.ShapeDtypeStruct((supernodes, width, span), jnp.bfloat16),
        ),
        in_specs=[smem, smem, smem, vmem, anywhere, anywhere],
        out_specs=(vmem, vmem, vmem),
        scratch_shapes=[
            pltpu.VMEM((n, ancestor_rows.shape[2] // (2 * width), width, 2 * width), jnp.bfloat16)
            for _ in range(poles)
        ]
        + [
            pltpu.VMEM(factor_rows.shape, jnp.bfloat16),
            pltpu.VMEM(diag_inverse.shape, jnp.float32),
            pltpu.VMEM((supernodes, poles, width, 2 * blocks * width), jnp.bfloat16),
            pltpu.VMEM((supernodes, width, span), jnp.float32),
            pltpu.SemaphoreType.DMA((4, n, poles)),
            pltpu.SemaphoreType.DMA((n, poles)),
            pltpu.SemaphoreType.DMA((2,)),
        ],
        compiler_params=pltpu.CompilerParams(
            collective_id=0, has_side_effects=True, vmem_limit_bytes=VMEM_BYTES
        ),
    )(pattern, lengths, pole_weight, ancestor_rows, factor_rows, diag_inverse)


def slot_layout(pattern, lengths, devices_total, capacity):
    supernodes, blocks = pattern.shape
    live_slots = jnp.arange(blocks)[None, :] < lengths[:, None]
    targets = pattern.reshape(-1)
    live_flat = live_slots.reshape(-1)
    pair_total = supernodes * blocks
    positions = jnp.arange(pair_total)
    earlier = (
        (targets[:, None] == targets[None, :])
        & live_flat[None, :]
        & (positions[None, :] < positions[:, None])
    )
    ranking = jnp.sum(earlier, axis=1)
    slot_total = devices_total * capacity
    slot_of_pair = jnp.where(live_flat, targets * capacity + ranking, slot_total)
    matches = jnp.arange(slot_total)[:, None] == slot_of_pair[None, :]
    source_pair = jnp.sum(jnp.where(matches, positions[None, :], 0), axis=1)
    occupied = jnp.any(matches, axis=1)
    return (live_slots, live_flat, slot_of_pair, source_pair // blocks, occupied)


def routed(ancestor_rows, factor_rows, pattern, lengths, diag_inverse, pole_weight):
    supernodes, pole_count, block_width, row_span = factor_rows.shape
    blocks = pattern.shape[1]
    devices_total = lax.axis_size("col")
    capacity = CAP
    slot_total = devices_total * capacity
    live_slots, live_flat, slot_of_pair, source_super, occupied = slot_layout(
        pattern, lengths, devices_total, capacity
    )
    live_columns = jnp.repeat(live_slots, block_width, axis=1).astype(jnp.bfloat16)
    masked_factor = factor_rows * live_columns[:, None, None, :]
    ancestors = ancestor_rows.shape[2] // block_width
    request = jnp.where(occupied[:, None], jnp.take(pattern, source_super, axis=0), 0)
    request = request.reshape(devices_total, capacity, blocks)
    clipped = jnp.minimum(slot_of_pair, slot_total - 1)
    table = ancestor_rows.reshape(pole_count, block_width, ancestors, block_width)
    outgoing = jnp.take(masked_factor, source_super, axis=0)
    outgoing = outgoing.reshape(devices_total, capacity, pole_count, block_width, row_span)
    factor_part = lax.all_to_all(outgoing, "col", split_axis=0, concat_axis=0, tiled=True)
    indices = lax.all_to_all(request, "col", split_axis=0, concat_axis=0, tiled=True)
    peer_count = indices.shape[0]
    slot_depth = indices.shape[1]
    gathered = jnp.take(table, indices, axis=2)
    gathered = gathered.reshape(
        pole_count, block_width, peer_count, slot_depth, blocks * block_width
    )
    products = jnp.einsum(
        "ncpix,pjncx->ncipj", factor_part, gathered, preferred_element_type=jnp.float32
    )
    rounded = products.astype(jnp.bfloat16).reshape(
        peer_count, slot_depth, block_width, pole_count * block_width
    )
    returned = lax.all_to_all(rounded, "col", split_axis=0, concat_axis=0, tiled=True)
    per_pair = jnp.take(
        returned.reshape(slot_total, block_width, pole_count, block_width), clipped, axis=0
    )
    per_pair = per_pair * live_flat.astype(jnp.bfloat16)[:, None, None, None]
    column_blocks = jnp.transpose(
        per_pair.reshape(supernodes, blocks, block_width, pole_count, block_width), (0, 3, 2, 1, 4)
    )
    column_blocks = column_blocks.reshape(supernodes, pole_count, block_width, row_span)
    inverse_row = -column_blocks
    diagonal = jnp.einsum(
        "kpic,kpjc->kipj", masked_factor, column_blocks, preferred_element_type=jnp.float32
    )
    inverse_diag = diag_inverse + diagonal.reshape(
        supernodes, block_width, pole_count * block_width
    )
    density = -jnp.sum(pole_weight[None, :, None, None] * column_blocks.astype(jnp.float32), axis=1)
    return (inverse_row, inverse_diag, density.astype(jnp.bfloat16))


def shards(ancestor_rows, *others):
    n = lax.axis_size("col")
    if n % 4 == 0 and n * ancestor_rows.size * ancestor_rows.dtype.itemsize <= TABLE_BYTES:
        return gathered(ancestor_rows, *others)
    return routed(ancestor_rows, *others)


def solution(mesh):
    placed = (
        P("kpt", "col", None),
        P("col", "kpt", None, None),
        P("col", None),
        P("col"),
        P("col", "kpt", None),
        P(),
    )
    return jax.shard_map(
        shards,
        mesh=mesh,
        in_specs=placed,
        out_specs=(P("col", "kpt", None, None), P("col", "kpt", None), P("col", "kpt", None)),
        check_vma=False,
    )
```

```python
import functools

import jax
import jax.numpy as jnp
from jax import lax
from jax.experimental import pallas as pl
from jax.experimental.pallas import tpu as pltpu
from jax.sharding import PartitionSpec as P

CAP = 2
MESH = pl.DeviceIdType.MESH
TABLE_BYTES = 16 * 2**20
VMEM_BYTES = 60 * 2**20
LEFT, RIGHT, ACROSS, TWIN = range(4)


def gather_kernel(
    line,
    pattern, lengths, weight, anc_hbm, factor_hbm, diag_hbm,
    row_out, diag_out, density_out,
    *scratch,
):
    poles, width, span = anc_hbm.shape
    tables = scratch[:poles]
    anc, factor, diag, spread, partial, send_sem, recv_sem, local_sem = scratch[poles:]
    supernodes = factor.shape[0]
    blocks = pattern.shape[0]
    me = lax.axis_index("col")
    core, row, z = me % 2, (me // 2) % 2, me // 4

    def index(at_z, at_row, at_core):
        return (at_z * 2 + at_row) * 2 + at_core

    targets = {
        LEFT: index(z - 1, row, core),
        RIGHT: index(z + 1, row, core),
        ACROSS: index(z, 1 - row, core),
        TWIN: index(z, row, 1 - core),
    }
    has = {LEFT: z > 0, RIGHT: z < line - 1}

    factor_in = pltpu.make_async_copy(factor_hbm, factor, local_sem.at[0])
    diag_in = pltpu.make_async_copy(diag_hbm, diag, local_sem.at[1])
    anc_in = pltpu.make_async_copy(anc_hbm, anc, local_sem.at[2])
    anc_in.start()
    factor_in.start()
    diag_in.start()

    barrier = pltpu.get_barrier_semaphore()

    def greet(way):
        pl.semaphore_signal(barrier, inc=1, device_id={"col": targets[way]}, device_id_type=MESH)

    greet(TWIN)
    greet(ACROSS)
    for way in (LEFT, RIGHT):
        pl.when(has[way])(functools.partial(greet, way))
    anc_in.wait()
    for p in range(poles):
        for strip in range(span // (2 * width)):
            tables[p][me, strip] = anc[p, :, strip * 2 * width:(strip + 1) * 2 * width]
    pl.semaphore_wait(barrier, 2 + has[LEFT].astype(jnp.int32) + has[RIGHT].astype(jnp.int32))

    def remote(way, origin, p, source):
        return pltpu.make_async_remote_copy(
            src_ref=source,
            dst_ref=tables[p].at[origin],
            send_sem=send_sem.at[way, origin, p],
            recv_sem=recv_sem.at[origin, p],
            device_id={"col": targets[way]},
            device_id_type=MESH,
        )

    def send(way, origin, p, source):
        remote(way, origin, p, source).start()

    def arrived(origin, p):
        remote(TWIN, origin, p, tables[p].at[origin]).wait_recv()

    def own(p):
        block = tables[p].at[me]
        for way in (LEFT, RIGHT):
            pl.when(has[way])(functools.partial(send, way, me, p, block))
        send(ACROSS, me, p, block)
        send(TWIN, me, p, block)

    def by_line(at_z, p):
        return ((at_z == 0) | (at_z == line - 1)) & (p == poles - 1)

    def from_line(p, side, distance):
        at_z = z - distance if side == LEFT else z + distance
        inside = at_z >= 0 if side == LEFT else at_z < line
        onward = RIGHT if side == LEFT else LEFT

        @pl.when(inside)
        def _():
            origin = index(at_z, row, core)
            arrived(origin, p)
            block = tables[p].at[origin]
            pl.when(has[onward])(functools.partial(send, onward, origin, p, block))
            pl.when(jnp.logical_not(by_line(at_z, p)))(functools.partial(send, ACROSS, origin, p, block))
            send(TWIN, origin, p, block)

    def from_other_line(p, side, distance):
        at_z = z - distance if side == LEFT else z + distance
        inside = at_z >= 0 if side == LEFT else at_z < line
        onward = RIGHT if side == LEFT else LEFT

        @pl.when(inside & by_line(at_z, p))
        def _():
            origin = index(at_z, 1 - row, core)
            arrived(origin, p)
            block = tables[p].at[origin]
            pl.when(has[onward])(functools.partial(send, onward, origin, p, block))
            send(TWIN, origin, p, block)

    def from_across(p, distance):
        for sign in (-1, 1) if distance else (1,):
            at_z = z + sign * distance

            crosses = (at_z >= 0) & (at_z < line)
            if distance:
                crosses = crosses & jnp.logical_not(by_line(at_z, p))

            @pl.when(crosses)
            def _():
                origin = index(at_z, 1 - row, core)
                arrived(origin, p)
                block = tables[p].at[origin]
                if not distance:
                    for way in (LEFT, RIGHT):
                        pl.when(has[way] & by_line(z, p))(functools.partial(send, way, origin, p, block))
                send(TWIN, origin, p, block)

    def from_twin(p):
        for at_z in range(line):
            for at_row in range(2):
                arrived(index(at_z, at_row, 1 - core), p)

    lane = lax.broadcasted_iota(jnp.int32, (width, 2 * width), 1)

    def prepare():
        for k in range(supernodes):
            length = jnp.full(lane.shape, lengths[k], jnp.int32)
            for p in range(poles):
                for s in range(blocks):
                    start = s // 2 * 2 * width
                    strip = factor[k, p, :, start:start + 2 * width].astype(jnp.float32)
                    half = jnp.full(lane.shape, lax.rem(pattern[s, k], 2), jnp.int32)
                    swapped = jnp.concatenate([strip[:, width:], strip[:, :width]], axis=1)
                    placed = jnp.where(half == s % 2, strip, swapped)
                    keep = (lane // width == half) & (s < length)
                    spread[k, p, :, s * 2 * width:(s + 1) * 2 * width] = jnp.where(
                        keep, placed, 0.0
                    ).astype(jnp.bfloat16)

    wide = lax.broadcasted_iota(jnp.int32, (width, blocks * width), 1)
    contract = (((1,), (1,)), ((), ()))

    def compute(p):
        columns = slice(p * width, (p + 1) * width)
        products, terms = [], []
        for k in range(supernodes):
            strips = [lax.div(pattern[s, k], 2) for s in range(blocks)]
            picked = jnp.concatenate(
                [
                    jnp.concatenate([tables[p][pattern[r, k], strip] for strip in strips], axis=1)
                    for r in range(blocks)
                ],
                axis=0,
            )
            product = lax.dot_general(spread[k, p], picked, contract, preferred_element_type=jnp.float32)
            live = wide < jnp.full(wide.shape, lengths[k] * width, jnp.int32)
            products.append(jnp.where(live, product, 0.0).astype(jnp.bfloat16))
        for k in range(supernodes):
            terms.append(
                lax.dot_general(factor[k, p], products[k], contract, preferred_element_type=jnp.float32)
            )
        for k in range(supernodes):
            row_out[k, p] = -products[k]
            total = weight[p] * products[k].astype(jnp.float32)
            if p > 0:
                total = partial[k] + total
            if p < poles - 1:
                partial[k] = total
            else:
                density_out[k] = (-total).astype(jnp.bfloat16)
        for k in range(supernodes):
            diag_out[k, :, columns] = diag[k, :, columns] + terms[k]

    for p in range(poles):
        own(p)
    factor_in.wait()
    diag_in.wait()
    prepare()
    last = poles - 1
    steps = []
    for p in range(poles):
        for distance in range(1, line):
            for side in (LEFT, RIGHT):
                steps.append((poles * (distance - 1) + p, 0, functools.partial(from_line, p, side, distance)))
                if p == last:
                    steps.append((poles * distance, -1, functools.partial(from_other_line, p, side, distance)))
        for distance in range(line):
            steps.append((poles * distance + p, 1, functools.partial(from_across, p, distance)))
    for _, _, step in sorted(steps, key=lambda entry: entry[:2]):
        step()
    for p in range(poles):
        from_twin(p)
        compute(p)

    def left_device(way, origin, p):
        remote(way, origin, p, tables[p].at[origin]).wait_send()

    for p in range(poles):
        for at_z in range(line):
            origin = index(at_z, row, core)
            pl.when(has[LEFT] & (at_z >= z))(functools.partial(left_device, LEFT, origin, p))
            pl.when(has[RIGHT] & (at_z <= z))(functools.partial(left_device, RIGHT, origin, p))
            pl.when(jnp.logical_not(by_line(at_z, p)) | (z == at_z))(functools.partial(left_device, ACROSS, origin, p))
            other = index(at_z, 1 - row, core)
            pl.when(has[LEFT] & (at_z >= z) & by_line(at_z, p))(functools.partial(left_device, LEFT, other, p))
            pl.when(has[RIGHT] & (at_z <= z) & by_line(at_z, p))(functools.partial(left_device, RIGHT, other, p))
            for at_row in range(2):
                left_device(TWIN, index(at_z, at_row, core), p)


def write_kernel(*refs):
    count = len(refs) // 3
    sources, targets, held, sem = refs[:count], refs[count:2 * count], refs[2 * count:3 * count], refs[-1]
    copies = []
    for i in range(count):
        for k in range(sources[i].shape[0]):
            loads = pltpu.make_async_copy(sources[i].at[k], held[i].at[k], sem.at[i, k, 0])
            stores = pltpu.make_async_copy(held[i].at[k], targets[i].at[k], sem.at[i, k, 1])
            copies.append((loads, stores))
            loads.start()
    for loads, stores in copies:
        loads.wait()
        stores.start()
    for _, stores in copies:
        stores.wait()


def gathered(ancestor_rows, factor_rows, pattern, lengths, diag_inverse, pole_weight):
    supernodes, poles, width, span = factor_rows.shape
    n = lax.axis_size("col")
    blocks = pattern.shape[1]
    smem = pl.BlockSpec(memory_space=pltpu.SMEM)
    vmem = pl.BlockSpec(memory_space=pltpu.VMEM)
    anywhere = pl.BlockSpec(memory_space=pl.ANY)
    results = pl.pallas_call(
        functools.partial(gather_kernel, n // 4),
        out_shape=(
            jax.ShapeDtypeStruct(factor_rows.shape, jnp.bfloat16),
            jax.ShapeDtypeStruct(diag_inverse.shape, jnp.float32),
            jax.ShapeDtypeStruct((supernodes, width, span), jnp.bfloat16),
        ),
        in_specs=[smem, smem, smem, anywhere, anywhere, anywhere],
        out_specs=(vmem, vmem, vmem),
        scratch_shapes=[
            pltpu.VMEM((n, ancestor_rows.shape[2] // (2 * width), width, 2 * width), jnp.bfloat16)
            for _ in range(poles)
        ]
        + [
            pltpu.VMEM(ancestor_rows.shape, jnp.bfloat16),
            pltpu.VMEM(factor_rows.shape, jnp.bfloat16),
            pltpu.VMEM(diag_inverse.shape, jnp.float32),
            pltpu.VMEM((supernodes, poles, width, 2 * blocks * width), jnp.bfloat16),
            pltpu.VMEM((supernodes, width, span), jnp.float32),
            pltpu.SemaphoreType.DMA((4, n, poles)),
            pltpu.SemaphoreType.DMA((n, poles)),
            pltpu.SemaphoreType.DMA((3,)),
        ],
        compiler_params=pltpu.CompilerParams(
            collective_id=0, has_side_effects=True, vmem_limit_bytes=VMEM_BYTES
        ),
    )(pattern.T, lengths, pole_weight, ancestor_rows, factor_rows, diag_inverse)
    return pl.pallas_call(
        write_kernel,
        out_shape=tuple(jax.ShapeDtypeStruct(x.shape, x.dtype) for x in results),
        in_specs=[anywhere] * 3,
        out_specs=(anywhere,) * 3,
        scratch_shapes=[pltpu.VMEM(x.shape, x.dtype) for x in results]
        + [pltpu.SemaphoreType.DMA((3, supernodes, 2))],
    )(*results)


def slot_layout(pattern, lengths, devices_total, capacity):
    supernodes, blocks = pattern.shape
    live_slots = jnp.arange(blocks)[None, :] < lengths[:, None]
    targets = pattern.reshape(-1)
    live_flat = live_slots.reshape(-1)
    pair_total = supernodes * blocks
    positions = jnp.arange(pair_total)
    earlier = (
        (targets[:, None] == targets[None, :])
        & live_flat[None, :]
        & (positions[None, :] < positions[:, None])
    )
    ranking = jnp.sum(earlier, axis=1)
    slot_total = devices_total * capacity
    slot_of_pair = jnp.where(live_flat, targets * capacity + ranking, slot_total)
    matches = jnp.arange(slot_total)[:, None] == slot_of_pair[None, :]
    source_pair = jnp.sum(jnp.where(matches, positions[None, :], 0), axis=1)
    occupied = jnp.any(matches, axis=1)
    return (live_slots, live_flat, slot_of_pair, source_pair // blocks, occupied)


def routed(ancestor_rows, factor_rows, pattern, lengths, diag_inverse, pole_weight):
    supernodes, pole_count, block_width, row_span = factor_rows.shape
    blocks = pattern.shape[1]
    devices_total = lax.axis_size("col")
    capacity = CAP
    slot_total = devices_total * capacity
    live_slots, live_flat, slot_of_pair, source_super, occupied = slot_layout(
        pattern, lengths, devices_total, capacity
    )
    live_columns = jnp.repeat(live_slots, block_width, axis=1).astype(jnp.bfloat16)
    masked_factor = factor_rows * live_columns[:, None, None, :]
    ancestors = ancestor_rows.shape[2] // block_width
    request = jnp.where(occupied[:, None], jnp.take(pattern, source_super, axis=0), 0)
    request = request.reshape(devices_total, capacity, blocks)
    clipped = jnp.minimum(slot_of_pair, slot_total - 1)
    table = ancestor_rows.reshape(pole_count, block_width, ancestors, block_width)
    outgoing = jnp.take(masked_factor, source_super, axis=0)
    outgoing = outgoing.reshape(devices_total, capacity, pole_count, block_width, row_span)
    factor_part = lax.all_to_all(outgoing, "col", split_axis=0, concat_axis=0, tiled=True)
    indices = lax.all_to_all(request, "col", split_axis=0, concat_axis=0, tiled=True)
    peer_count = indices.shape[0]
    slot_depth = indices.shape[1]
    gathered = jnp.take(table, indices, axis=2)
    gathered = gathered.reshape(
        pole_count, block_width, peer_count, slot_depth, blocks * block_width
    )
    products = jnp.einsum(
        "ncpix,pjncx->ncipj", factor_part, gathered, preferred_element_type=jnp.float32
    )
    rounded = products.astype(jnp.bfloat16).reshape(
        peer_count, slot_depth, block_width, pole_count * block_width
    )
    returned = lax.all_to_all(rounded, "col", split_axis=0, concat_axis=0, tiled=True)
    per_pair = jnp.take(
        returned.reshape(slot_total, block_width, pole_count, block_width), clipped, axis=0
    )
    per_pair = per_pair * live_flat.astype(jnp.bfloat16)[:, None, None, None]
    column_blocks = jnp.transpose(
        per_pair.reshape(supernodes, blocks, block_width, pole_count, block_width), (0, 3, 2, 1, 4)
    )
    column_blocks = column_blocks.reshape(supernodes, pole_count, block_width, row_span)
    inverse_row = -column_blocks
    diagonal = jnp.einsum(
        "kpic,kpjc->kipj", masked_factor, column_blocks, preferred_element_type=jnp.float32
    )
    inverse_diag = diag_inverse + diagonal.reshape(
        supernodes, block_width, pole_count * block_width
    )
    density = -jnp.sum(pole_weight[None, :, None, None] * column_blocks.astype(jnp.float32), axis=1)
    return (inverse_row, inverse_diag, density.astype(jnp.bfloat16))


def shards(ancestor_rows, *others):
    n = lax.axis_size("col")
    if n % 4 == 0 and n * ancestor_rows.size * ancestor_rows.dtype.itemsize <= TABLE_BYTES:
        return gathered(ancestor_rows, *others)
    return routed(ancestor_rows, *others)


def solution(mesh):
    placed = (
        P("kpt", "col", None),
        P("col", "kpt", None, None),
        P("col", None),
        P("col"),
        P("col", "kpt", None),
        P(),
    )
    return jax.shard_map(
        shards,
        mesh=mesh,
        in_specs=placed,
        out_specs=(P("col", "kpt", None, None), P("col", "kpt", None), P("col", "kpt", None)),
        check_vma=False,
    )
```

```python
import functools

import jax
import jax.numpy as jnp
from jax import lax
from jax.experimental import pallas as pl
from jax.experimental.pallas import tpu as pltpu
from jax.sharding import PartitionSpec as P

CAP = 2
MESH = pl.DeviceIdType.MESH
TABLE_BYTES = 16 * 2**20
VMEM_BYTES = 60 * 2**20
LEFT, RIGHT, ACROSS, TWIN = range(4)


def gather_kernel(
    line,
    pattern_hbm, lengths_hbm, weight_hbm, anc_hbm, factor_hbm, diag_hbm,
    row_out, diag_out, density_out,
    *scratch,
):
    poles, width, span = anc_hbm.shape
    tables = scratch[:poles]
    pattern, lengths, weight, anc, factor, diag, spread, partial = scratch[poles:poles + 8]
    send_sem, recv_sem, local_sem = scratch[poles + 8:]
    supernodes = factor.shape[0]
    blocks = pattern.shape[0]
    me = lax.axis_index("col")
    core, row, z = me % 2, (me // 2) % 2, me // 4

    def index(at_z, at_row, at_core):
        return (at_z * 2 + at_row) * 2 + at_core

    targets = {
        LEFT: index(z - 1, row, core),
        RIGHT: index(z + 1, row, core),
        ACROSS: index(z, 1 - row, core),
        TWIN: index(z, row, 1 - core),
    }
    has = {LEFT: z > 0, RIGHT: z < line - 1}

    pairs = (
        (anc_hbm, anc), (pattern_hbm, pattern), (lengths_hbm, lengths), (weight_hbm, weight),
        (factor_hbm, factor), (diag_hbm, diag),
    )
    incoming = [pltpu.make_async_copy(a, b, local_sem.at[i]) for i, (a, b) in enumerate(pairs)]
    for copy in incoming:
        copy.start()

    barrier = pltpu.get_barrier_semaphore()

    def greet(way):
        pl.semaphore_signal(barrier, inc=1, device_id={"col": targets[way]}, device_id_type=MESH)

    greet(TWIN)
    greet(ACROSS)
    for way in (LEFT, RIGHT):
        pl.when(has[way])(functools.partial(greet, way))
    incoming[0].wait()
    for p in range(poles):
        for strip in range(span // (2 * width)):
            tables[p][me, strip] = anc[p, :, strip * 2 * width:(strip + 1) * 2 * width]
    pl.semaphore_wait(barrier, 2 + has[LEFT].astype(jnp.int32) + has[RIGHT].astype(jnp.int32))

    def remote(way, origin, p, source):
        return pltpu.make_async_remote_copy(
            src_ref=source,
            dst_ref=tables[p].at[origin],
            send_sem=send_sem.at[way, origin, p],
            recv_sem=recv_sem.at[origin, p],
            device_id={"col": targets[way]},
            device_id_type=MESH,
        )

    def send(way, origin, p, source):
        remote(way, origin, p, source).start()

    def arrived(origin, p):
        remote(TWIN, origin, p, tables[p].at[origin]).wait_recv()

    def own(p):
        block = tables[p].at[me]
        for way in (LEFT, RIGHT):
            pl.when(has[way])(functools.partial(send, way, me, p, block))
        send(ACROSS, me, p, block)
        send(TWIN, me, p, block)

    def by_line(at_z, p):
        return ((at_z == 0) | (at_z == line - 1)) & (p == poles - 1)

    def from_line(p, side, distance):
        at_z = z - distance if side == LEFT else z + distance
        inside = at_z >= 0 if side == LEFT else at_z < line
        onward = RIGHT if side == LEFT else LEFT

        @pl.when(inside)
        def _():
            origin = index(at_z, row, core)
            arrived(origin, p)
            block = tables[p].at[origin]
            pl.when(has[onward])(functools.partial(send, onward, origin, p, block))
            pl.when(jnp.logical_not(by_line(at_z, p)))(functools.partial(send, ACROSS, origin, p, block))
            send(TWIN, origin, p, block)

    def from_other_line(p, side, distance):
        at_z = z - distance if side == LEFT else z + distance
        inside = at_z >= 0 if side == LEFT else at_z < line
        onward = RIGHT if side == LEFT else LEFT

        @pl.when(inside & by_line(at_z, p))
        def _():
            origin = index(at_z, 1 - row, core)
            arrived(origin, p)
            block = tables[p].at[origin]
            pl.when(has[onward])(functools.partial(send, onward, origin, p, block))
            send(TWIN, origin, p, block)

    def from_across(p, distance):
        for sign in (-1, 1) if distance else (1,):
            at_z = z + sign * distance

            crosses = (at_z >= 0) & (at_z < line)
            if distance:
                crosses = crosses & jnp.logical_not(by_line(at_z, p))

            @pl.when(crosses)
            def _():
                origin = index(at_z, 1 - row, core)
                arrived(origin, p)
                block = tables[p].at[origin]
                if not distance:
                    for way in (LEFT, RIGHT):
                        pl.when(has[way] & by_line(z, p))(functools.partial(send, way, origin, p, block))
                send(TWIN, origin, p, block)

    def from_twin(p):
        for at_z in range(line):
            for at_row in range(2):
                arrived(index(at_z, at_row, 1 - core), p)

    lane = lax.broadcasted_iota(jnp.int32, (width, 2 * width), 1)

    def prepare():
        for k in range(supernodes):
            length = jnp.full(lane.shape, lengths[k], jnp.int32)
            for p in range(poles):
                for s in range(blocks):
                    start = s // 2 * 2 * width
                    strip = factor[k, p, :, start:start + 2 * width].astype(jnp.float32)
                    half = jnp.full(lane.shape, lax.rem(pattern[s, k], 2), jnp.int32)
                    swapped = jnp.concatenate([strip[:, width:], strip[:, :width]], axis=1)
                    placed = jnp.where(half == s % 2, strip, swapped)
                    keep = (lane // width == half) & (s < length)
                    spread[k, p, :, s * 2 * width:(s + 1) * 2 * width] = jnp.where(
                        keep, placed, 0.0
                    ).astype(jnp.bfloat16)

    last = poles - 1
    wide = lax.broadcasted_iota(jnp.int32, (width, blocks * width), 1)
    contract = (((1,), (1,)), ((), ()))

    def compute(p):
        columns = slice(p * width, (p + 1) * width)
        products, terms = [], []
        for k in range(supernodes):
            strips = [lax.div(pattern[s, k], 2) for s in range(blocks)]
            picked = jnp.concatenate(
                [
                    jnp.concatenate([tables[p][pattern[r, k], strip] for strip in strips], axis=1)
                    for r in range(blocks)
                ],
                axis=0,
            )
            product = lax.dot_general(spread[k, p], picked, contract, preferred_element_type=jnp.float32)
            live = wide < jnp.full(wide.shape, lengths[k] * width, jnp.int32)
            products.append(jnp.where(live, product, 0.0).astype(jnp.bfloat16))
        for k in range(supernodes):
            terms.append(
                lax.dot_general(factor[k, p], products[k], contract, preferred_element_type=jnp.float32)
            )
        for k in range(supernodes):
            row_out[k, p] = -products[k]
            total = weight[p] * products[k].astype(jnp.float32)
            if p > 0:
                total = partial[k] + total
            if p < poles - 1:
                partial[k] = total
            else:
                density_out[k] = (-total).astype(jnp.bfloat16)
        for k in range(supernodes):
            diag_out[k, :, columns] = diag[k, :, columns] + terms[k]

    for p in range(poles):
        own(p)
    for copy in incoming[1:]:
        copy.wait()
    prepare()
    steps = []
    for p in range(poles):
        for distance in range(1, line):
            for side in (LEFT, RIGHT):
                steps.append((poles * (distance - 1) + p, 0, functools.partial(from_line, p, side, distance)))
                if p == last:
                    steps.append((poles * distance, -1, functools.partial(from_other_line, p, side, distance)))
        for distance in range(line):
            steps.append((poles * distance + p, 1, functools.partial(from_across, p, distance)))
    for _, _, step in sorted(steps, key=lambda entry: entry[:2]):
        step()
    for p in range(poles):
        from_twin(p)
        compute(p)

    def left_device(way, origin, p):
        remote(way, origin, p, tables[p].at[origin]).wait_send()

    for p in range(poles):
        for at_z in range(line):
            origin = index(at_z, row, core)
            pl.when(has[LEFT] & (at_z >= z))(functools.partial(left_device, LEFT, origin, p))
            pl.when(has[RIGHT] & (at_z <= z))(functools.partial(left_device, RIGHT, origin, p))
            pl.when(jnp.logical_not(by_line(at_z, p)) | (z == at_z))(functools.partial(left_device, ACROSS, origin, p))
            other = index(at_z, 1 - row, core)
            pl.when(has[LEFT] & (at_z >= z) & by_line(at_z, p))(functools.partial(left_device, LEFT, other, p))
            pl.when(has[RIGHT] & (at_z <= z) & by_line(at_z, p))(functools.partial(left_device, RIGHT, other, p))
            for at_row in range(2):
                left_device(TWIN, index(at_z, at_row, core), p)


def write_kernel(*refs):
    count = len(refs) // 2
    sources, targets, sem = refs[:count], refs[count:2 * count], refs[-1]
    copies = [pltpu.make_async_copy(a, b, sem.at[i]) for i, (a, b) in enumerate(zip(sources, targets))]
    for copy in copies:
        copy.start()
    for copy in copies:
        copy.wait()


def gathered(ancestor_rows, factor_rows, pattern, lengths, diag_inverse, pole_weight):
    supernodes, poles, width, span = factor_rows.shape
    n = lax.axis_size("col")
    blocks = pattern.shape[1]
    anywhere = pl.BlockSpec(memory_space=pl.ANY)
    vmem = pl.BlockSpec(memory_space=pltpu.VMEM)
    results = pl.pallas_call(
        functools.partial(gather_kernel, n // 4),
        out_shape=(
            pltpu.VMEM(factor_rows.shape, jnp.bfloat16),
            pltpu.VMEM(diag_inverse.shape, jnp.float32),
            pltpu.VMEM((supernodes, width, span), jnp.bfloat16),
        ),
        in_specs=[anywhere] * 6,
        out_specs=(vmem,) * 3,
        scratch_shapes=[
            pltpu.VMEM((n, ancestor_rows.shape[2] // (2 * width), width, 2 * width), jnp.bfloat16)
            for _ in range(poles)
        ]
        + [
            pltpu.SMEM((blocks, supernodes), jnp.int32),
            pltpu.SMEM(lengths.shape, jnp.int32),
            pltpu.SMEM(pole_weight.shape, jnp.float32),
            pltpu.VMEM(ancestor_rows.shape, jnp.bfloat16),
            pltpu.VMEM(factor_rows.shape, jnp.bfloat16),
            pltpu.VMEM(diag_inverse.shape, jnp.float32),
            pltpu.VMEM((supernodes, poles, width, 2 * blocks * width), jnp.bfloat16),
            pltpu.VMEM((supernodes, width, span), jnp.float32),
            pltpu.SemaphoreType.DMA((4, n, poles)),
            pltpu.SemaphoreType.DMA((n, poles)),
            pltpu.SemaphoreType.DMA((6,)),
        ],
        compiler_params=pltpu.CompilerParams(
            collective_id=0, has_side_effects=True, vmem_limit_bytes=VMEM_BYTES
        ),
    )(pattern.T, lengths, pole_weight, ancestor_rows, factor_rows, diag_inverse)
    results = [pltpu.with_memory_space_constraint(x, pltpu.VMEM) for x in results]
    return pl.pallas_call(
        write_kernel,
        out_shape=tuple(jax.ShapeDtypeStruct(x.shape, x.dtype) for x in results),
        in_specs=[vmem] * 3,
        out_specs=(anywhere,) * 3,
        scratch_shapes=[pltpu.SemaphoreType.DMA((3,))],
    )(*results)


def slot_layout(pattern, lengths, devices_total, capacity):
    supernodes, blocks = pattern.shape
    live_slots = jnp.arange(blocks)[None, :] < lengths[:, None]
    targets = pattern.reshape(-1)
    live_flat = live_slots.reshape(-1)
    pair_total = supernodes * blocks
    positions = jnp.arange(pair_total)
    earlier = (
        (targets[:, None] == targets[None, :])
        & live_flat[None, :]
        & (positions[None, :] < positions[:, None])
    )
    ranking = jnp.sum(earlier, axis=1)
    slot_total = devices_total * capacity
    slot_of_pair = jnp.where(live_flat, targets * capacity + ranking, slot_total)
    matches = jnp.arange(slot_total)[:, None] == slot_of_pair[None, :]
    source_pair = jnp.sum(jnp.where(matches, positions[None, :], 0), axis=1)
    occupied = jnp.any(matches, axis=1)
    return (live_slots, live_flat, slot_of_pair, source_pair // blocks, occupied)


def routed(ancestor_rows, factor_rows, pattern, lengths, diag_inverse, pole_weight):
    supernodes, pole_count, block_width, row_span = factor_rows.shape
    blocks = pattern.shape[1]
    devices_total = lax.axis_size("col")
    capacity = CAP
    slot_total = devices_total * capacity
    live_slots, live_flat, slot_of_pair, source_super, occupied = slot_layout(
        pattern, lengths, devices_total, capacity
    )
    live_columns = jnp.repeat(live_slots, block_width, axis=1).astype(jnp.bfloat16)
    masked_factor = factor_rows * live_columns[:, None, None, :]
    ancestors = ancestor_rows.shape[2] // block_width
    request = jnp.where(occupied[:, None], jnp.take(pattern, source_super, axis=0), 0)
    request = request.reshape(devices_total, capacity, blocks)
    clipped = jnp.minimum(slot_of_pair, slot_total - 1)
    table = ancestor_rows.reshape(pole_count, block_width, ancestors, block_width)
    outgoing = jnp.take(masked_factor, source_super, axis=0)
    outgoing = outgoing.reshape(devices_total, capacity, pole_count, block_width, row_span)
    factor_part = lax.all_to_all(outgoing, "col", split_axis=0, concat_axis=0, tiled=True)
    indices = lax.all_to_all(request, "col", split_axis=0, concat_axis=0, tiled=True)
    peer_count = indices.shape[0]
    slot_depth = indices.shape[1]
    gathered = jnp.take(table, indices, axis=2)
    gathered = gathered.reshape(
        pole_count, block_width, peer_count, slot_depth, blocks * block_width
    )
    products = jnp.einsum(
        "ncpix,pjncx->ncipj", factor_part, gathered, preferred_element_type=jnp.float32
    )
    rounded = products.astype(jnp.bfloat16).reshape(
        peer_count, slot_depth, block_width, pole_count * block_width
    )
    returned = lax.all_to_all(rounded, "col", split_axis=0, concat_axis=0, tiled=True)
    per_pair = jnp.take(
        returned.reshape(slot_total, block_width, pole_count, block_width), clipped, axis=0
    )
    per_pair = per_pair * live_flat.astype(jnp.bfloat16)[:, None, None, None]
    column_blocks = jnp.transpose(
        per_pair.reshape(supernodes, blocks, block_width, pole_count, block_width), (0, 3, 2, 1, 4)
    )
    column_blocks = column_blocks.reshape(supernodes, pole_count, block_width, row_span)
    inverse_row = -column_blocks
    diagonal = jnp.einsum(
        "kpic,kpjc->kipj", masked_factor, column_blocks, preferred_element_type=jnp.float32
    )
    inverse_diag = diag_inverse + diagonal.reshape(
        supernodes, block_width, pole_count * block_width
    )
    density = -jnp.sum(pole_weight[None, :, None, None] * column_blocks.astype(jnp.float32), axis=1)
    return (inverse_row, inverse_diag, density.astype(jnp.bfloat16))


def shards(ancestor_rows, *others):
    n = lax.axis_size("col")
    if n % 4 == 0 and n * ancestor_rows.size * ancestor_rows.dtype.itemsize <= TABLE_BYTES:
        return gathered(ancestor_rows, *others)
    return routed(ancestor_rows, *others)


def solution(mesh):
    placed = (
        P("kpt", "col", None),
        P("col", "kpt", None, None),
        P("col", None),
        P("col"),
        P("col", "kpt", None),
        P(),
    )
    return jax.shard_map(
        shards,
        mesh=mesh,
        in_specs=placed,
        out_specs=(P("col", "kpt", None, None), P("col", "kpt", None), P("col", "kpt", None)),
        check_vma=False,
    )
```

```python
import functools

import jax
import jax.numpy as jnp
from jax import lax
from jax.experimental import pallas as pl
from jax.experimental.pallas import tpu as pltpu
from jax.sharding import PartitionSpec as P

CAP = 2
MESH = pl.DeviceIdType.MESH
TABLE_BYTES = 16 * 2**20
VMEM_BYTES = 60 * 2**20
LEFT, RIGHT, ACROSS, TWIN = range(4)


def gather_kernel(
    line,
    pattern_hbm, lengths_hbm, weight_hbm, anc_hbm, factor_hbm, diag_hbm,
    row_out, diag_out, density_out,
    *scratch,
):
    poles, width, span = anc_hbm.shape
    tables = scratch[:poles]
    pattern, lengths, weight, anc, factor, diag, spread, partial = scratch[poles:poles + 8]
    send_sem, recv_sem, local_sem = scratch[poles + 8:]
    supernodes = factor.shape[0]
    blocks = pattern.shape[0]
    me = lax.axis_index("col")
    core, row, z = me % 2, (me // 2) % 2, me // 4

    def index(at_z, at_row, at_core):
        return (at_z * 2 + at_row) * 2 + at_core

    targets = {
        LEFT: index(z - 1, row, core),
        RIGHT: index(z + 1, row, core),
        ACROSS: index(z, 1 - row, core),
        TWIN: index(z, row, 1 - core),
    }
    has = {LEFT: z > 0, RIGHT: z < line - 1}

    pairs = (
        (anc_hbm, anc), (pattern_hbm, pattern), (lengths_hbm, lengths), (weight_hbm, weight),
        (factor_hbm, factor), (diag_hbm, diag),
    )
    incoming = [pltpu.make_async_copy(a, b, local_sem.at[i]) for i, (a, b) in enumerate(pairs)]
    incoming[0].start()

    barrier = pltpu.get_barrier_semaphore()

    def greet(way):
        pl.semaphore_signal(barrier, inc=1, device_id={"col": targets[way]}, device_id_type=MESH)

    greet(TWIN)
    greet(ACROSS)
    for way in (LEFT, RIGHT):
        pl.when(has[way])(functools.partial(greet, way))
    for copy in incoming[1:]:
        copy.start()

    def lay_out(p):
        for strip in range(span // (2 * width)):
            tables[p][me, strip] = anc[p, :, strip * 2 * width:(strip + 1) * 2 * width]

    incoming[0].wait()
    lay_out(0)
    pl.semaphore_wait(barrier, 2 + has[LEFT].astype(jnp.int32) + has[RIGHT].astype(jnp.int32))

    def remote(way, origin, p, source):
        return pltpu.make_async_remote_copy(
            src_ref=source,
            dst_ref=tables[p].at[origin],
            send_sem=send_sem.at[way, origin, p],
            recv_sem=recv_sem.at[origin, p],
            device_id={"col": targets[way]},
            device_id_type=MESH,
        )

    def send(way, origin, p, source):
        remote(way, origin, p, source).start()

    def arrived(origin, p):
        remote(TWIN, origin, p, tables[p].at[origin]).wait_recv()

    def own(p):
        block = tables[p].at[me]
        for way in (LEFT, RIGHT):
            pl.when(has[way])(functools.partial(send, way, me, p, block))
        send(ACROSS, me, p, block)
        send(TWIN, me, p, block)

    def by_line(at_z, p):
        return ((at_z == 0) | (at_z == line - 1)) & (p == poles - 1)

    def from_line(p, side, distance):
        at_z = z - distance if side == LEFT else z + distance
        inside = at_z >= 0 if side == LEFT else at_z < line
        onward = RIGHT if side == LEFT else LEFT

        @pl.when(inside)
        def _():
            origin = index(at_z, row, core)
            arrived(origin, p)
            block = tables[p].at[origin]
            pl.when(has[onward])(functools.partial(send, onward, origin, p, block))
            pl.when(jnp.logical_not(by_line(at_z, p)))(functools.partial(send, ACROSS, origin, p, block))
            send(TWIN, origin, p, block)

    def from_other_line(p, side, distance):
        at_z = z - distance if side == LEFT else z + distance
        inside = at_z >= 0 if side == LEFT else at_z < line
        onward = RIGHT if side == LEFT else LEFT

        @pl.when(inside & by_line(at_z, p))
        def _():
            origin = index(at_z, 1 - row, core)
            arrived(origin, p)
            block = tables[p].at[origin]
            pl.when(has[onward])(functools.partial(send, onward, origin, p, block))
            send(TWIN, origin, p, block)

    def from_across(p, distance):
        for sign in (-1, 1) if distance else (1,):
            at_z = z + sign * distance

            crosses = (at_z >= 0) & (at_z < line)
            if distance:
                crosses = crosses & jnp.logical_not(by_line(at_z, p))

            @pl.when(crosses)
            def _():
                origin = index(at_z, 1 - row, core)
                arrived(origin, p)
                block = tables[p].at[origin]
                if not distance:
                    for way in (LEFT, RIGHT):
                        pl.when(has[way] & by_line(z, p))(functools.partial(send, way, origin, p, block))
                send(TWIN, origin, p, block)

    def from_twin(p):
        for at_z in range(line):
            for at_row in range(2):
                arrived(index(at_z, at_row, 1 - core), p)

    lane = lax.broadcasted_iota(jnp.int32, (width, 2 * width), 1)

    def prepare():
        for k in range(supernodes):
            length = jnp.full(lane.shape, lengths[k], jnp.int32)
            for p in range(poles):
                for s in range(blocks):
                    start = s // 2 * 2 * width
                    strip = factor[k, p, :, start:start + 2 * width].astype(jnp.float32)
                    half = jnp.full(lane.shape, lax.rem(pattern[s, k], 2), jnp.int32)
                    swapped = jnp.concatenate([strip[:, width:], strip[:, :width]], axis=1)
                    placed = jnp.where(half == s % 2, strip, swapped)
                    keep = (lane // width == half) & (s < length)
                    spread[k, p, :, s * 2 * width:(s + 1) * 2 * width] = jnp.where(
                        keep, placed, 0.0
                    ).astype(jnp.bfloat16)

    last = poles - 1
    wide = lax.broadcasted_iota(jnp.int32, (width, blocks * width), 1)
    contract = (((1,), (1,)), ((), ()))

    def compute(p):
        columns = slice(p * width, (p + 1) * width)
        products, terms = [], []
        for k in range(supernodes):
            strips = [lax.div(pattern[s, k], 2) for s in range(blocks)]
            picked = jnp.concatenate(
                [
                    jnp.concatenate([tables[p][pattern[r, k], strip] for strip in strips], axis=1)
                    for r in range(blocks)
                ],
                axis=0,
            )
            product = lax.dot_general(spread[k, p], picked, contract, preferred_element_type=jnp.float32)
            live = wide < jnp.full(wide.shape, lengths[k] * width, jnp.int32)
            products.append(jnp.where(live, product, 0.0).astype(jnp.bfloat16))
        for k in range(supernodes):
            terms.append(
                lax.dot_general(factor[k, p], products[k], contract, preferred_element_type=jnp.float32)
            )
        for k in range(supernodes):
            row_out[k, p] = -products[k]
            total = weight[p] * products[k].astype(jnp.float32)
            if p > 0:
                total = partial[k] + total
            if p < poles - 1:
                partial[k] = total
            else:
                density_out[k] = (-total).astype(jnp.bfloat16)
        for k in range(supernodes):
            diag_out[k, :, columns] = diag[k, :, columns] + terms[k]

    own(0)
    for p in range(1, poles):
        lay_out(p)
        own(p)
    for copy in incoming[1:]:
        copy.wait()
    steps = []
    for p in range(poles):
        for distance in range(1, line):
            for side in (LEFT, RIGHT):
                steps.append((poles * (distance - 1) + p, 0, functools.partial(from_line, p, side, distance)))
                if p == last:
                    steps.append((poles * distance, -1, functools.partial(from_other_line, p, side, distance)))
        for distance in range(line):
            steps.append((poles * distance + p, 1, functools.partial(from_across, p, distance)))
    steps.append((1, 5, prepare))
    for _, _, step in sorted(steps, key=lambda entry: entry[:2]):
        step()
    for p in range(poles):
        from_twin(p)
        compute(p)

    def left_device(way, origin, p):
        remote(way, origin, p, tables[p].at[origin]).wait_send()

    for p in range(poles):
        for at_z in range(line):
            origin = index(at_z, row, core)
            pl.when(has[LEFT] & (at_z >= z))(functools.partial(left_device, LEFT, origin, p))
            pl.when(has[RIGHT] & (at_z <= z))(functools.partial(left_device, RIGHT, origin, p))
            pl.when(jnp.logical_not(by_line(at_z, p)) | (z == at_z))(functools.partial(left_device, ACROSS, origin, p))
            other = index(at_z, 1 - row, core)
            pl.when(has[LEFT] & (at_z >= z) & by_line(at_z, p))(functools.partial(left_device, LEFT, other, p))
            pl.when(has[RIGHT] & (at_z <= z) & by_line(at_z, p))(functools.partial(left_device, RIGHT, other, p))
            for at_row in range(2):
                left_device(TWIN, index(at_z, at_row, core), p)


def write_kernel(*refs):
    count = len(refs) // 2
    sources, targets, sem = refs[:count], refs[count:2 * count], refs[-1]
    copies = [pltpu.make_async_copy(a, b, sem.at[i]) for i, (a, b) in enumerate(zip(sources, targets))]
    for copy in copies:
        copy.start()
    for copy in copies:
        copy.wait()


def gathered(ancestor_rows, factor_rows, pattern, lengths, diag_inverse, pole_weight):
    supernodes, poles, width, span = factor_rows.shape
    n = lax.axis_size("col")
    blocks = pattern.shape[1]
    anywhere = pl.BlockSpec(memory_space=pl.ANY)
    vmem = pl.BlockSpec(memory_space=pltpu.VMEM)
    results = pl.pallas_call(
        functools.partial(gather_kernel, n // 4),
        out_shape=(
            pltpu.VMEM(factor_rows.shape, jnp.bfloat16),
            pltpu.VMEM(diag_inverse.shape, jnp.float32),
            pltpu.VMEM((supernodes, width, span), jnp.bfloat16),
        ),
        in_specs=[anywhere] * 6,
        out_specs=(vmem,) * 3,
        scratch_shapes=[
            pltpu.VMEM((n, ancestor_rows.shape[2] // (2 * width), width, 2 * width), jnp.bfloat16)
            for _ in range(poles)
        ]
        + [
            pltpu.SMEM((blocks, supernodes), jnp.int32),
            pltpu.SMEM(lengths.shape, jnp.int32),
            pltpu.SMEM(pole_weight.shape, jnp.float32),
            pltpu.VMEM(ancestor_rows.shape, jnp.bfloat16),
            pltpu.VMEM(factor_rows.shape, jnp.bfloat16),
            pltpu.VMEM(diag_inverse.shape, jnp.float32),
            pltpu.VMEM((supernodes, poles, width, 2 * blocks * width), jnp.bfloat16),
            pltpu.VMEM((supernodes, width, span), jnp.float32),
            pltpu.SemaphoreType.DMA((4, n, poles)),
            pltpu.SemaphoreType.DMA((n, poles)),
            pltpu.SemaphoreType.DMA((6,)),
        ],
        compiler_params=pltpu.CompilerParams(
            collective_id=0, has_side_effects=True, vmem_limit_bytes=VMEM_BYTES
        ),
    )(pattern.T, lengths, pole_weight, ancestor_rows, factor_rows, diag_inverse)
    results = [pltpu.with_memory_space_constraint(x, pltpu.VMEM) for x in results]
    return pl.pallas_call(
        write_kernel,
        out_shape=tuple(jax.ShapeDtypeStruct(x.shape, x.dtype) for x in results),
        in_specs=[vmem] * 3,
        out_specs=(anywhere,) * 3,
        scratch_shapes=[pltpu.SemaphoreType.DMA((3,))],
    )(*results)


def slot_layout(pattern, lengths, devices_total, capacity):
    supernodes, blocks = pattern.shape
    live_slots = jnp.arange(blocks)[None, :] < lengths[:, None]
    targets = pattern.reshape(-1)
    live_flat = live_slots.reshape(-1)
    pair_total = supernodes * blocks
    positions = jnp.arange(pair_total)
    earlier = (
        (targets[:, None] == targets[None, :])
        & live_flat[None, :]
        & (positions[None, :] < positions[:, None])
    )
    ranking = jnp.sum(earlier, axis=1)
    slot_total = devices_total * capacity
    slot_of_pair = jnp.where(live_flat, targets * capacity + ranking, slot_total)
    matches = jnp.arange(slot_total)[:, None] == slot_of_pair[None, :]
    source_pair = jnp.sum(jnp.where(matches, positions[None, :], 0), axis=1)
    occupied = jnp.any(matches, axis=1)
    return (live_slots, live_flat, slot_of_pair, source_pair // blocks, occupied)


def routed(ancestor_rows, factor_rows, pattern, lengths, diag_inverse, pole_weight):
    supernodes, pole_count, block_width, row_span = factor_rows.shape
    blocks = pattern.shape[1]
    devices_total = lax.axis_size("col")
    capacity = CAP
    slot_total = devices_total * capacity
    live_slots, live_flat, slot_of_pair, source_super, occupied = slot_layout(
        pattern, lengths, devices_total, capacity
    )
    live_columns = jnp.repeat(live_slots, block_width, axis=1).astype(jnp.bfloat16)
    masked_factor = factor_rows * live_columns[:, None, None, :]
    ancestors = ancestor_rows.shape[2] // block_width
    request = jnp.where(occupied[:, None], jnp.take(pattern, source_super, axis=0), 0)
    request = request.reshape(devices_total, capacity, blocks)
    clipped = jnp.minimum(slot_of_pair, slot_total - 1)
    table = ancestor_rows.reshape(pole_count, block_width, ancestors, block_width)
    outgoing = jnp.take(masked_factor, source_super, axis=0)
    outgoing = outgoing.reshape(devices_total, capacity, pole_count, block_width, row_span)
    factor_part = lax.all_to_all(outgoing, "col", split_axis=0, concat_axis=0, tiled=True)
    indices = lax.all_to_all(request, "col", split_axis=0, concat_axis=0, tiled=True)
    peer_count = indices.shape[0]
    slot_depth = indices.shape[1]
    gathered = jnp.take(table, indices, axis=2)
    gathered = gathered.reshape(
        pole_count, block_width, peer_count, slot_depth, blocks * block_width
    )
    products = jnp.einsum(
        "ncpix,pjncx->ncipj", factor_part, gathered, preferred_element_type=jnp.float32
    )
    rounded = products.astype(jnp.bfloat16).reshape(
        peer_count, slot_depth, block_width, pole_count * block_width
    )
    returned = lax.all_to_all(rounded, "col", split_axis=0, concat_axis=0, tiled=True)
    per_pair = jnp.take(
        returned.reshape(slot_total, block_width, pole_count, block_width), clipped, axis=0
    )
    per_pair = per_pair * live_flat.astype(jnp.bfloat16)[:, None, None, None]
    column_blocks = jnp.transpose(
        per_pair.reshape(supernodes, blocks, block_width, pole_count, block_width), (0, 3, 2, 1, 4)
    )
    column_blocks = column_blocks.reshape(supernodes, pole_count, block_width, row_span)
    inverse_row = -column_blocks
    diagonal = jnp.einsum(
        "kpic,kpjc->kipj", masked_factor, column_blocks, preferred_element_type=jnp.float32
    )
    inverse_diag = diag_inverse + diagonal.reshape(
        supernodes, block_width, pole_count * block_width
    )
    density = -jnp.sum(pole_weight[None, :, None, None] * column_blocks.astype(jnp.float32), axis=1)
    return (inverse_row, inverse_diag, density.astype(jnp.bfloat16))


def shards(ancestor_rows, *others):
    n = lax.axis_size("col")
    if n % 4 == 0 and n * ancestor_rows.size * ancestor_rows.dtype.itemsize <= TABLE_BYTES:
        return gathered(ancestor_rows, *others)
    return routed(ancestor_rows, *others)


def solution(mesh):
    placed = (
        P("kpt", "col", None),
        P("col", "kpt", None, None),
        P("col", None),
        P("col"),
        P("col", "kpt", None),
        P(),
    )
    return jax.shard_map(
        shards,
        mesh=mesh,
        in_specs=placed,
        out_specs=(P("col", "kpt", None, None), P("col", "kpt", None), P("col", "kpt", None)),
        check_vma=False,
    )
```
